32 devices in a mesh: seq: 16 (over z, x, core), head: 2 (over y).
Axes of the slice: x: 2, y: 2, z: 4, core: 2. Of those that a mesh axis runs over, the one named last changes fastest.
Arguments:
- queries: bfloat16 [2048, 1024], P('seq', 'head'), may hold values from -8 to 8
- keys: bfloat16 [2048, 1024], P('seq', 'head'), may hold values from -8 to 8
- values: bfloat16 [2048, 1024], P('seq', 'head'), may hold values from -8 to 8
- w_out: bfloat16 [1024, 1024], P('head'), may hold values from -0.1875 to 0.1875
- d_mixed: bfloat16 [2048, 1024], P('seq'), may hold values from -6 to 6
Outputs:
- mixed: bfloat16 [2048, 1024], P(('seq', 'head'))
- d_queries: bfloat16 [2048, 1024], P('seq', 'head')
- d_keys: bfloat16 [2048, 1024], P('seq', 'head')
- d_values: bfloat16 [2048, 1024], P('seq', 'head')
The draws below stay inside these ranges and needn't reach their ends.
All inputs are finite; a program needn't handle non-finite values.
Results may differ from the reference program's by a relative error of at most 0.0074.
Values may be sent and summed in bfloat16 or wider, within the bound.
A program may use at most 64 MiB of HBM per device.

```python
import math
import jax
import jax.numpy as jnp
from jax import lax

D = 1024
HEAD_DIM = 64
BLOCK = 64
TOK_DEV = 128
TOKENS = 2048
REMOTE = 4
N_SEQ = 16


def layered(key, rough_scale):
    total = rough_scale * jax.random.normal(jax.random.fold_in(key, 0), (TOKENS, D), jnp.float32)
    shift_bits = BLOCK.bit_length() - 1
    layer_idx = 1
    while 1 << shift_bits < TOKENS:
        coarse = jax.random.normal(jax.random.fold_in(key, layer_idx), (TOKENS >> shift_bits, D), jnp.float32)
        total = total + 0.45 * jnp.repeat(coarse, 1 << shift_bits, axis=0)
        shift_bits = shift_bits + 2
        layer_idx = layer_idx + 1
    return total


def draw_queries(key, part):
    base_draw = layered(jax.random.fold_in(key, 1), 0.7)
    return jnp.clip(base_draw, -8.0, 8.0).astype(jnp.bfloat16)


def draw_keys(key, part):
    base_draw = layered(jax.random.fold_in(key, 2), 0.7)
    return jnp.clip(base_draw, -8.0, 8.0).astype(jnp.bfloat16)


def draw_values(key, part):
    base_draw = layered(jax.random.fold_in(key, 3), 0.7)
    return jnp.clip(base_draw, -8.0, 8.0).astype(jnp.bfloat16)


def levels(rng, shape, shards, low, high):
    level = 1.0
    for axis_at, blocks in shards:
        steps = jax.random.uniform(jax.random.fold_in(jax.random.fold_in(rng, 6), axis_at), (blocks,), jnp.float32, low / len(shards), high / len(shards))
        level = level * jnp.repeat(jnp.exp(steps), shape[axis_at] // blocks).reshape((-1,) + (1,) * (len(shape) - 1 - axis_at))
    return level


def normal_values(key, shape, width, reach, pieces=(), held_as=jnp.bfloat16):
    gain = levels(key, shape, pieces, -0.22, 0.18) if pieces else 1.0
    entries = jax.random.normal(key, shape, jnp.float32) * width * gain
    return jnp.minimum(jnp.maximum(entries, -reach), reach).astype(held_as)


def setup_inputs(seed: int = 0) -> dict:
    splits = jax.random.split(jax.random.key(seed), 6)
    return {
        "queries": draw_queries(jax.random.fold_in(splits[5], 71), 0),
        "keys": draw_keys(jax.random.fold_in(splits[5], 71), 0),
        "values": draw_values(jax.random.fold_in(splits[5], 71), 0),
        "w_out": normal_values(splits[3], (D, D), D ** -0.5, 0.1875, ((0, 2),)),
        "d_mixed": normal_values(splits[4], (TOKENS, D), 1.0, 6.0, ((0, 16),)),
    }


def score_product(form, left, right):
    return jnp.einsum(form, left.astype(jnp.float32), right.astype(jnp.float32))

def sibling_keys(central, block_length, group_len):
    row_share, feature_share = central.shape
    span_count = row_share // (block_length * group_len)
    pooled = lax.optimization_barrier(jnp.mean(central.reshape(span_count, block_length, group_len, feature_share), axis=2, dtype=jnp.float32))
    flipped = pooled.reshape(span_count // 2, 2, block_length, feature_share)[:, ::-1].reshape(span_count, block_length, feature_share)
    return jnp.repeat(flipped.astype(jnp.bfloat16), group_len, axis=0)

def fine_sets(source, row_share, block_length):
    count_of_blocks = row_share // block_length
    feature_share = source.shape[1]
    return jnp.concatenate([source[:row_share].reshape(count_of_blocks, block_length, feature_share), source[block_length:block_length + row_share].reshape(count_of_blocks, block_length, feature_share), source[2 * block_length:].reshape(count_of_blocks, block_length, feature_share)], axis=1)

def key_sets(source, far_source, block_length):
    row_share = source.shape[0] - 2 * block_length
    count_of_blocks = row_share // block_length
    feature_share = source.shape[1]
    levels_here = count_of_blocks.bit_length() - 2
    target = [fine_sets(source, row_share, block_length)]
    for level_idx in range(1, levels_here + 1):
        target.append(sibling_keys(source[block_length:block_length + row_share], block_length, 2 ** level_idx))
    far_flat = far_source.astype(jnp.bfloat16).reshape(-1, feature_share)
    target.append(jnp.broadcast_to(far_flat[None], (count_of_blocks, far_flat.shape[0], feature_share)))
    return jnp.concatenate(target, axis=1)

def return_scatter(grad_sets, row_share, block_length):
    count_of_blocks, total_key_count, feature_share = grad_sets.shape
    levels_here = count_of_blocks.bit_length() - 2
    grad_rows = jnp.pad(grad_sets[:, :block_length].reshape(row_share, feature_share), ((0, 2 * block_length), (0, 0)))
    grad_rows = grad_rows + jnp.pad(grad_sets[:, block_length:2 * block_length].reshape(row_share, feature_share), ((block_length, block_length), (0, 0)))
    grad_rows = grad_rows + jnp.pad(grad_sets[:, 2 * block_length:3 * block_length].reshape(row_share, feature_share), ((2 * block_length, 0), (0, 0)))
    central_extra = jnp.zeros((row_share, feature_share), jnp.float32)
    offset = 3 * block_length
    for level_idx in range(1, levels_here + 1):
        group_len = 2 ** level_idx
        span_count = row_share // (block_length * group_len)
        level_grad = grad_sets[:, offset:offset + block_length]
        summed = level_grad.reshape(span_count, group_len, block_length, feature_share).sum(axis=1)
        owner_grad = summed.reshape(span_count // 2, 2, block_length, feature_share)[:, ::-1].reshape(span_count, block_length, feature_share)
        spread = jnp.broadcast_to((owner_grad / group_len)[:, :, None, :], (span_count, block_length, group_len, feature_share))
        central_extra = central_extra + spread.reshape(row_share, feature_share)
        offset = offset + block_length
    far_grad = grad_sets[:, offset:].sum(axis=0).reshape(-1, block_length, feature_share)
    grad_rows = grad_rows + jnp.pad(central_extra, ((block_length, block_length), (0, 0)))
    return (grad_rows, far_grad)

def attend(query_rows, keys_ext, values_ext, far_keys, far_values, grad_attn, at_start, at_end, block_length, head_dim):
    row_share, feature_share = query_rows.shape
    count_of_blocks = row_share // block_length
    head_count = feature_share // head_dim
    key_all = key_sets(keys_ext, far_keys, block_length)
    value_all = key_sets(values_ext, far_values, block_length)
    total_key_count = key_all.shape[1]
    query_blocks = query_rows.reshape(count_of_blocks, block_length, head_count, head_dim)
    key_blocks = key_all.reshape(count_of_blocks, total_key_count, head_count, head_dim)
    value_blocks = value_all.reshape(count_of_blocks, total_key_count, head_count, head_dim)
    inv_scale = 1.0 / math.sqrt(head_dim)
    scores = score_product('nqhd,nkhd->nhqk', query_blocks, key_blocks) * inv_scale
    column = lax.broadcasted_iota(jnp.int32, (count_of_blocks, total_key_count), 1)
    block_ids = lax.broadcasted_iota(jnp.int32, (count_of_blocks, total_key_count), 0)
    blocked = (block_ids == 0) & (column < block_length) & at_start | (block_ids == count_of_blocks - 1) & (column >= 2 * block_length) & (column < 3 * block_length) & at_end
    scores = jnp.where(blocked[:, None, None, :], -jnp.inf, scores)
    row_max = lax.optimization_barrier(jnp.max(scores, axis=-1, keepdims=True))
    exp_terms = jnp.exp(scores - row_max)
    normed = exp_terms / lax.optimization_barrier(jnp.sum(exp_terms, axis=-1, keepdims=True))
    softmax_weights = normed.astype(jnp.bfloat16)
    attention_layer = score_product('nhqk,nkhd->nqhd', softmax_weights, value_blocks).reshape(row_share, feature_share).astype(jnp.bfloat16)
    gradient_blocks = grad_attn.reshape(count_of_blocks, block_length, head_count, head_dim)
    grad_normed = score_product('nqhd,nkhd->nhqk', gradient_blocks, value_blocks)
    inner_sum = lax.optimization_barrier(jnp.sum(normed * grad_normed, axis=-1, keepdims=True))
    grad_scores = (normed * (grad_normed - inner_sum) * inv_scale).astype(jnp.bfloat16)
    query_gradient = score_product('nhqk,nkhd->nqhd', grad_scores, key_blocks).reshape(row_share, feature_share)
    grad_kset = score_product('ueji,ujeo->uieo', grad_scores, query_blocks).reshape(count_of_blocks, total_key_count, feature_share)
    value_set_gradient = score_product('ueji,ujeo->uieo', softmax_weights, gradient_blocks).reshape(count_of_blocks, total_key_count, feature_share)
    extended_key_gradient, remote_key_gradient = return_scatter(grad_kset, row_share, block_length)
    extended_value_gradient, remote_value_gradient = return_scatter(value_set_gradient, row_share, block_length)
    return (attention_layer, query_gradient, extended_key_gradient, extended_value_gradient, remote_key_gradient, remote_value_gradient)

def reference(queries, keys, values, w_out, d_mixed):
    row_share = TOK_DEV
    block_length = BLOCK
    grad_attn = jnp.dot(d_mixed.astype(jnp.float32), w_out.astype(jnp.float32).T, preferred_element_type=jnp.float32).astype(jnp.bfloat16)
    tables_k = []
    tables_v = []
    for bit_level in range(REMOTE):
        span_rows = row_share * 2 ** bit_level
        tables_k.append(lax.optimization_barrier(jnp.mean(keys.reshape(TOKENS // span_rows, block_length, span_rows // block_length, D), axis=2, dtype=jnp.float32)))
        tables_v.append(lax.optimization_barrier(jnp.mean(values.reshape(TOKENS // span_rows, block_length, span_rows // block_length, D), axis=2, dtype=jnp.float32)))
    keys_pad = jnp.pad(keys, ((block_length, block_length), (0, 0)))
    values_pad = jnp.pad(values, ((block_length, block_length), (0, 0)))

    def per_stretch(stretch_idx):
        span_start = stretch_idx * row_share
        query_rows = lax.dynamic_slice_in_dim(queries, span_start, row_share, 0)
        keys_ext = lax.dynamic_slice_in_dim(keys_pad, span_start, row_share + 2 * block_length, 0)
        values_ext = lax.dynamic_slice_in_dim(values_pad, span_start, row_share + 2 * block_length, 0)
        grad_rows = lax.dynamic_slice_in_dim(grad_attn, span_start, row_share, 0)
        far_keys = jnp.stack([lax.dynamic_index_in_dim(table_k, (stretch_idx >> bit_level ^ 1).astype(jnp.int32), 0, keepdims=False) for bit_level, table_k in enumerate(tables_k)])
        far_values = jnp.stack([lax.dynamic_index_in_dim(table_v, (stretch_idx >> bit_level ^ 1).astype(jnp.int32), 0, keepdims=False) for bit_level, table_v in enumerate(tables_v)])
        return attend(query_rows, keys_ext, values_ext, far_keys, far_values, grad_rows, stretch_idx == 0, stretch_idx == N_SEQ - 1, block_length, HEAD_DIM)
    stretch_outputs = lax.map(per_stretch, jnp.arange(N_SEQ, dtype=jnp.int32))
    attention_layer, query_gradient, extended_key_gradient, extended_value_gradient, remote_key_gradient, remote_value_gradient = stretch_outputs
    attention_layer = attention_layer.reshape(TOKENS, D)
    mixed = jnp.dot(attention_layer.astype(jnp.float32), w_out.astype(jnp.float32), preferred_element_type=jnp.float32).astype(jnp.bfloat16)
    layer_results = []
    for extended_gradient, remote_gradient in ((extended_key_gradient, remote_key_gradient), (extended_value_gradient, remote_value_gradient)):
        central = extended_gradient[:, block_length:block_length + row_share]
        central = central.at[:-1, row_share - block_length:].add(extended_gradient[1:, :block_length])
        central = central.at[1:, :block_length].add(extended_gradient[:-1, block_length + row_share:])
        central = central.reshape(TOKENS, D)
        for bit_level in range(REMOTE):
            span_count = N_SEQ >> bit_level
            span_rows = row_share * 2 ** bit_level
            group_len = span_rows // block_length
            summed = remote_gradient[:, bit_level].reshape(span_count, 2 ** bit_level, block_length, D).sum(axis=1)
            owner_grad = summed.reshape(span_count // 2, 2, block_length, D)[:, ::-1].reshape(span_count, block_length, D)
            spread = jnp.broadcast_to((owner_grad / group_len)[:, :, None, :], (span_count, block_length, group_len, D))
            central = central + spread.reshape(TOKENS, D)
        layer_results.append(central.astype(jnp.bfloat16))
    return (mixed, query_gradient.reshape(TOKENS, D).astype(jnp.bfloat16), layer_results[0], layer_results[1])
```

```python
import functools

import jax
import jax.numpy as jnp
from jax import lax
from jax.experimental import pallas as pl
from jax.experimental.pallas import tpu as pltpu
from jax.sharding import PartitionSpec as P

HEAD_DIM = 64
BLOCK = 64
ROWS = 128
PAIR = 2 * HEAD_DIM
HALO = 2 * BLOCK
FAR = HALO + ROWS
MESH = pl.DeviceIdType.MESH
BF16 = jnp.bfloat16
F32 = jnp.float32


def dot_nt(left, right):
    return lax.dot_general(
        left, right, (((1,), (1,)), ((), ())), preferred_element_type=F32
    )


def dot_nn(left, right):
    return jnp.dot(left, right, preferred_element_type=F32)


def each(count, step):
    if count <= 8:
        for i in range(count):
            step(i)
    else:
        lax.fori_loop(0, count, lambda i, c: (step(i), c)[1], 0)


def group_matrix(shape, token_dim, rows, first):
    group = ROWS // rows
    token = lax.broadcasted_iota(jnp.int32, shape, token_dim)
    other = lax.broadcasted_iota(jnp.int32, shape, 1 - token_dim)
    return jnp.where(token // group + first == other, 1.0 / group, 0.0).astype(BF16)


def kernel(n_seq, levels, *refs):
    q_in, k_in, v_in, w_in, dm_in, mixed_out, dq_out, dk_out, dv_out = refs[:9]
    (
        q, w, dm, kv, dattn, attn, dq, bias, gown, hsend, hrecv, gsend, grecv,
        mix_send, mix_recv, mix_own, dkv_stage, mixed_stage,
        in_sem, out_sem, halo_s, halo_r, far_s, far_r,
        ghalo_s, ghalo_r, gfar_s, gfar_r, mix_sem,
    ) = refs[9:38]
    rest = refs[38:]
    psend = rest[:levels]
    n_small = max(levels - 3, 0)
    srecv = rest[levels : levels + n_small]
    gssend = rest[levels + n_small : levels + 2 * n_small]
    gsrecv = rest[levels + 2 * n_small :]
    feats = q.shape[1]
    big = min(levels, 3)
    me = lax.axis_index("seq")
    hd = lax.axis_index("head")
    other_head = 1 - hd

    loads = [
        pltpu.make_async_copy(k_in, kv.at[0, HALO:FAR], in_sem.at[0]),
        pltpu.make_async_copy(v_in, kv.at[1, HALO:FAR], in_sem.at[1]),
        pltpu.make_async_copy(dm_in, dm, in_sem.at[2]),
        pltpu.make_async_copy(w_in, w, in_sem.at[3]),
        pltpu.make_async_copy(q_in, q, in_sem.at[4]),
    ]
    for load in loads:
        load.start()

    barrier = pltpu.get_barrier_semaphore()

    def greet(i):
        pl.semaphore_signal(
            barrier, 1, device_id={"seq": (me + 1 + i) % n_seq}, device_id_type=MESH
        )

    lax.fori_loop(0, n_seq - 1, lambda i, c: (greet(i), c)[1], 0)
    pl.semaphore_signal(barrier, 1, device_id={"head": other_head}, device_id_type=MESH)

    @pl.when(me == 0)
    def _():
        kv[:, 0:BLOCK, :] = jnp.zeros((2, BLOCK, feats), BF16)
        hrecv[:, 0:BLOCK, :] = jnp.zeros((2, BLOCK, feats), BF16)

    @pl.when(me == n_seq - 1)
    def _():
        kv[:, BLOCK:HALO, :] = jnp.zeros((2, BLOCK, feats), BF16)
        hrecv[:, BLOCK:HALO, :] = jnp.zeros((2, BLOCK, feats), BF16)

    second = (lax.broadcasted_iota(jnp.int32, (8, 2 * ROWS), 1) // BLOCK) % 2
    missing = ((second == 0) & (me == 0)) | ((second == 1) & (me == n_seq - 1))
    bias[...] = jnp.where(missing, -jnp.inf, 0.0)

    loads[0].wait()
    loads[1].wait()

    spans = []
    for b in range(levels):
        size = 2**b
        span = me // size
        sibling = (span + 1 - 2 * (span % 2)) * size
        mine = me % size
        spans.append((size, BLOCK >> b, sibling, mine))

    k_own = kv[0, HALO:FAR, :]
    v_own = kv[1, HALO:FAR, :]
    for b, (size, rows, sibling, mine) in enumerate(spans):
        if b < 3:
            mat = group_matrix((rows, ROWS), 1, rows, 0)
            psend[b][0] = dot_nn(mat, k_own).astype(BF16)
            psend[b][1] = dot_nn(mat, v_own).astype(BF16)
        else:
            mat = group_matrix((8, ROWS), 1, rows, (mine * rows) % 8)
            psend[b][...] = jnp.concatenate(
                [dot_nn(mat, k_own), dot_nn(mat, v_own)], axis=0
            ).astype(BF16)

    pl.semaphore_wait(barrier, n_seq)

    def halo_copy(way):
        if way == 0:
            src, dst, to = kv.at[:, HALO + BLOCK : FAR], kv.at[:, 0:BLOCK], me + 1
        else:
            src, dst, to = kv.at[:, HALO : HALO + BLOCK], kv.at[:, BLOCK:HALO], me - 1
        return pltpu.make_async_remote_copy(
            src, dst, halo_s.at[way], halo_r.at[way],
            device_id={"seq": to}, device_id_type=MESH,
        )

    def far_copy(b, dest, slot):
        size, rows, sibling, mine = spans[b]
        if b < 3:
            dst = kv.at[:, pl.ds(pl.multiple_of(FAR + BLOCK * b + slot * rows, 16), rows)]
        else:
            dst = srecv[b - 3].at[slot]
        return pltpu.make_async_remote_copy(
            psend[b], dst, far_s.at[size - 1 + dest], far_r.at[size - 1 + slot],
            device_id={"seq": sibling + dest}, device_id_type=MESH,
        )

    for b in reversed(range(levels)):
        each(2**b, lambda i, b=b: far_copy(b, i, spans[b][3]).start())

    has_next = me < n_seq - 1
    has_prev = me > 0
    pl.when(has_next)(lambda: halo_copy(0).start())
    pl.when(has_prev)(lambda: halo_copy(1).start())

    loads[2].wait()
    loads[3].wait()
    dattn[...] = dot_nt(dm[...], w[...]).astype(BF16)
    loads[4].wait()

    pl.when(has_prev)(lambda: halo_copy(0).wait_recv())
    pl.when(has_next)(lambda: halo_copy(1).wait_recv())
    for b in range(levels):
        each(2**b, lambda i, b=b: far_copy(b, 0, i).wait_recv())

    for b in range(3, levels):
        rows = spans[b][1]
        per = 8 // rows
        pieces = []
        for g in range(8):
            total = srecv[b - 3][g * per].astype(F32)
            for s in range(1, per):
                total = total + srecv[b - 3][g * per + s].astype(F32)
            pieces.append(total)
        at = FAR + BLOCK * b
        for part in range(2):
            kv[part, at : at + BLOCK, :] = jnp.concatenate(
                [piece[8 * part : 8 * part + 8] for piece in pieces], axis=0
            ).astype(BF16)

    lane = lax.broadcasted_iota(jnp.int32, (1, PAIR), 1)
    head_a = jnp.where(lane < HEAD_DIM, 1.0, 0.0).astype(BF16)
    head_b = jnp.where(lane < HEAD_DIM, 0.0, 1.0).astype(BF16)
    token = (lax.broadcasted_iota(jnp.int32, (1, 2 * ROWS), 1) // BLOCK) % 2
    first = token == 0
    mask0 = jnp.where(first, 1.0, 0.0)
    mask1 = jnp.where(first, 0.0, 1.0)

    for pair in range(feats // PAIR):
        cols = slice(pair * PAIR, (pair + 1) * PAIR)
        qp = q[:, cols] * jnp.asarray(0.125, BF16)
        dap = dattn[:, cols]
        qs = jnp.concatenate([qp * head_a, qp * head_b], axis=0)
        das = jnp.concatenate([dap * head_a, dap * head_b], axis=0)
        kp = kv[0, :, cols]
        vp = kv[1, :, cols]

        def merge(full):
            halo = jnp.where(first, full[:BLOCK], full[BLOCK:HALO])
            return halo, full[HALO:]

        s_halo, s_rest = merge(dot_nt(kp, qs))
        s_all = jnp.concatenate([s_halo + bias[0:1, :], s_rest], axis=0)
        top = jnp.max(s_all, axis=0, keepdims=True)
        e_all = jnp.exp(s_all - top)
        normed = e_all * (1.0 / jnp.sum(e_all, axis=0, keepdims=True))

        def unmerge(full):
            halo = full[:BLOCK]
            return jnp.concatenate(
                [halo * mask0, halo * mask1, full[BLOCK:]], axis=0
            ).astype(BF16)

        weights = unmerge(normed)
        d_halo, d_rest = merge(dot_nt(vp, das))
        d_normed = jnp.concatenate([d_halo, d_rest], axis=0)
        inner = jnp.sum(normed * d_normed, axis=0, keepdims=True)
        d_scores = unmerge(normed * (d_normed - inner))

        def both(values_t, coeffs):
            full = dot_nn(values_t, coeffs)
            return jnp.concatenate(
                [full[:HEAD_DIM, :ROWS], full[HEAD_DIM:, ROWS:]], axis=0
            ).T

        attn[:, cols] = both(vp.T, weights).astype(BF16)
        dq[:, cols] = (both(kp.T, d_scores) * 0.125).astype(BF16)
        grads = (dot_nn(d_scores, qs), dot_nn(weights, das))
        for part in range(2):
            grad = grads[part]
            hsend[part, :, cols] = grad[:HALO].astype(BF16)
            gown[part, :, cols] = grad[HALO:FAR]
            gsend[part, :, cols] = grad[FAR : FAR + BLOCK * big].astype(BF16)
        for b in range(3, levels):
            at = FAR + BLOCK * b
            for g in range(8):
                gssend[b - 3][g, :, cols] = jnp.concatenate(
                    [grad[at + 8 * g : at + 8 * g + 8] for grad in grads], axis=0
                ).astype(BF16)

    def ghalo_copy(way):
        if way == 0:
            src, dst, to = hsend.at[:, 0:BLOCK], hrecv.at[:, BLOCK:HALO], me - 1
        else:
            src, dst, to = hsend.at[:, BLOCK:HALO], hrecv.at[:, 0:BLOCK], me + 1
        return pltpu.make_async_remote_copy(
            src, dst, ghalo_s.at[way], ghalo_r.at[way],
            device_id={"seq": to}, device_id_type=MESH,
        )

    def gfar_copy(b, dest, slot):
        size, rows, sibling, mine = spans[b]
        if b < 3:
            src = gsend.at[:, pl.ds(pl.multiple_of(BLOCK * b + dest * rows, 16), rows)]
            dst = grecv.at[:, pl.ds(pl.multiple_of(BLOCK * b + slot * rows, 16), rows)]
        else:
            src = gssend[b - 3].at[dest // (8 // rows)]
            dst = gsrecv[b - 3].at[slot]
        return pltpu.make_async_remote_copy(
            src, dst, gfar_s.at[size - 1 + dest], gfar_r.at[size - 1 + slot],
            device_id={"seq": sibling + dest}, device_id_type=MESH,
        )

    for b in reversed(range(levels)):
        each(2**b, lambda i, b=b: gfar_copy(b, i, spans[b][3]).start())
    pl.when(has_prev)(lambda: ghalo_copy(0).start())
    pl.when(has_next)(lambda: ghalo_copy(1).start())

    dq_store = pltpu.make_async_copy(dq, dq_out, out_sem.at[0])
    dq_store.start()

    theirs = pl.ds(pl.multiple_of(other_head * BLOCK, BLOCK), BLOCK)
    ours = pl.ds(pl.multiple_of(hd * BLOCK, BLOCK), BLOCK)
    mix_send[...] = dot_nn(attn[theirs, :], w[...]).astype(BF16)
    mix_copy = pltpu.make_async_remote_copy(
        mix_send, mix_recv, mix_sem.at[0], mix_sem.at[1],
        device_id={"head": other_head}, device_id_type=MESH,
    )
    mix_copy.start()
    mix_own[...] = dot_nn(attn[ours, :], w[...])

    pl.when(has_next)(lambda: ghalo_copy(0).wait_recv())
    pl.when(has_prev)(lambda: ghalo_copy(1).wait_recv())
    for b in range(levels):
        each(2**b, lambda i, b=b: gfar_copy(b, 0, i).wait_recv())

    stores = []
    for part in range(2):
        total = gown[part] + hrecv[part].astype(F32)
        for b, (size, rows, sibling, mine) in enumerate(spans):
            if b < 3:
                token = lax.broadcasted_iota(jnp.int32, (ROWS, BLOCK), 0)
                row = lax.broadcasted_iota(jnp.int32, (ROWS, BLOCK), 1)
                group = ROWS // rows
                mat = jnp.where(token // group == row % rows, 1.0 / group, 0.0).astype(BF16)
                total = total + dot_nn(mat, grecv[part, BLOCK * b : BLOCK * (b + 1), :])
            else:
                wide = 16 * size
                token = lax.broadcasted_iota(jnp.int32, (ROWS, wide), 0)
                row = lax.broadcasted_iota(jnp.int32, (ROWS, wide), 1) % 16
                group = ROWS // rows
                wanted = token // group + (mine * rows) % 8 + 8 * part
                mat = jnp.where(wanted == row, 1.0 / group, 0.0).astype(BF16)
                total = total + dot_nn(mat, gsrecv[b - 3][...].reshape(wide, feats))
        dkv_stage[part] = total.astype(BF16)
        store = pltpu.make_async_copy(
            dkv_stage.at[part], (dk_out, dv_out)[part], out_sem.at[1 + part]
        )
        store.start()
        stores.append(store)

    mix_copy.wait_recv()
    mixed_stage[...] = (mix_own[...] + mix_recv[...].astype(F32)).astype(BF16)
    mixed_store = pltpu.make_async_copy(mixed_stage, mixed_out, out_sem.at[3])
    mixed_store.start()

    pl.when(has_next)(lambda: halo_copy(0).wait_send())
    pl.when(has_prev)(lambda: halo_copy(1).wait_send())
    pl.when(has_prev)(lambda: ghalo_copy(0).wait_send())
    pl.when(has_next)(lambda: ghalo_copy(1).wait_send())
    for b in range(levels):
        each(2**b, lambda i, b=b: far_copy(b, i, spans[b][3]).wait_send())
        each(2**b, lambda i, b=b: gfar_copy(b, i, spans[b][3]).wait_send())
    mix_copy.wait_send()
    dq_store.wait()
    for store in stores:
        store.wait()
    mixed_store.wait()


def on_device(n_seq, queries, keys, values, w_out, d_mixed):
    feats = queries.shape[1]
    width = w_out.shape[1]
    levels = n_seq.bit_length() - 1
    big = min(levels, 3)
    small = list(range(3, levels))
    n_keys = FAR + BLOCK * levels
    vmem = pltpu.VMEM
    dma = pltpu.SemaphoreType.DMA
    scratch = [
        vmem((ROWS, feats), BF16),
        vmem((feats, width), BF16),
        vmem((ROWS, width), BF16),
        vmem((2, n_keys, feats), BF16),
        vmem((ROWS, feats), BF16),
        vmem((ROWS, feats), BF16),
        vmem((ROWS, feats), BF16),
        vmem((8, 2 * ROWS), F32),
        vmem((2, ROWS, feats), F32),
        vmem((2, HALO, feats), BF16),
        vmem((2, HALO, feats), BF16),
        vmem((2, BLOCK * big, feats), BF16),
        vmem((2, BLOCK * big, feats), BF16),
        vmem((BLOCK, width), BF16),
        vmem((BLOCK, width), BF16),
        vmem((BLOCK, width), F32),
        vmem((2, ROWS, feats), BF16),
        vmem((BLOCK, width), BF16),
        dma((5,)),
        dma((4,)),
        dma((2,)),
        dma((2,)),
        dma((n_seq - 1,)),
        dma((n_seq - 1,)),
        dma((2,)),
        dma((2,)),
        dma((n_seq - 1,)),
        dma((n_seq - 1,)),
        dma((2,)),
    ]
    scratch += [vmem((2, BLOCK >> b, feats), BF16) for b in range(big)]
    scratch += [vmem((16, feats), BF16) for b in small]
    scratch += [vmem((2**b, 16, feats), BF16) for b in small]
    scratch += [vmem((8, 16, feats), BF16) for b in small]
    scratch += [vmem((2**b, 16, feats), BF16) for b in small]
    anywhere = pl.BlockSpec(memory_space=pl.ANY)
    return pl.pallas_call(
        functools.partial(kernel, n_seq, levels),
        out_shape=[
            jax.ShapeDtypeStruct((BLOCK, width), BF16),
            jax.ShapeDtypeStruct((ROWS, feats), BF16),
            jax.ShapeDtypeStruct((ROWS, feats), BF16),
            jax.ShapeDtypeStruct((ROWS, feats), BF16),
        ],
        in_specs=[anywhere] * 5,
        out_specs=[anywhere] * 4,
        scratch_shapes=scratch,
        compiler_params=pltpu.CompilerParams(
            collective_id=0, has_side_effects=True, vmem_limit_bytes=40 * 2**20
        ),
    )(queries, keys, values, w_out, d_mixed)


def solution(mesh):
    in_specs = (
        P("seq", "head"),
        P("seq", "head"),
        P("seq", "head"),
        P("head", None),
        P("seq", None),
    )
    out_specs = (P(("seq", "head"), None), P("seq", "head"), P("seq", "head"), P("seq", "head"))
    return jax.shard_map(
        functools.partial(on_device, mesh.shape["seq"]),
        mesh=mesh,
        in_specs=in_specs,
        out_specs=out_specs,
        check_vma=False,
    )
```

```python
import functools

import jax
import jax.numpy as jnp
from jax import lax
from jax.experimental import pallas as pl
from jax.experimental.pallas import tpu as pltpu
from jax.sharding import PartitionSpec as P

HEAD_DIM = 64
BLOCK = 64
ROWS = 128
PAIR = 2 * HEAD_DIM
HALO = 2 * BLOCK
FAR = HALO + ROWS
MESH = pl.DeviceIdType.MESH
BF16 = jnp.bfloat16
F32 = jnp.float32


def dot_nt(left, right):
    return lax.dot_general(
        left, right, (((1,), (1,)), ((), ())), preferred_element_type=F32
    )


def dot_nn(left, right):
    return jnp.dot(left, right, preferred_element_type=F32)


def each(count, step):
    if count <= 8:
        for i in range(count):
            step(i)
    else:
        lax.fori_loop(0, count, lambda i, c: (step(i), c)[1], 0)


def group_matrix(shape, token_dim, rows, first):
    group = ROWS // rows
    token = lax.broadcasted_iota(jnp.int32, shape, token_dim)
    other = lax.broadcasted_iota(jnp.int32, shape, 1 - token_dim)
    return jnp.where(token // group + first == other, 1.0 / group, 0.0).astype(BF16)


def kernel(n_seq, levels, *refs):
    q_in, k_in, v_in, w_in, dm_in, mixed_out, dq, dk_out, dv_out = refs[:9]
    (
        q, w, dm, kv, dattn, attn, bias, gown, hsend, hrecv, gsend, grecv,
        mix_send, mix_recv, mix_own,
        in_sem, halo_s, halo_r, far_s, far_r,
        ghalo_s, ghalo_r, gfar_s, gfar_r, mix_sem,
        relay_s, relay_r, sum_s, sum_r, sum_recv, sum_send, small_recv, small_send,
    ) = refs[9:42]
    rest = refs[42:]
    psend = rest[:levels]
    n_small = max(levels - 3, 0)
    srecv = rest[levels : levels + n_small]
    gssend = rest[levels + n_small : levels + 2 * n_small]
    gsrecv = rest[levels + 2 * n_small :]
    feats = q.shape[1]
    big = min(levels, 3)
    me = lax.axis_index("seq")
    hd = lax.axis_index("head")
    other_head = 1 - hd
    core = me % 2
    twin = me + 1 - 2 * core

    loads = [
        pltpu.make_async_copy(k_in, kv.at[0, HALO:FAR], in_sem.at[0]),
        pltpu.make_async_copy(v_in, kv.at[1, HALO:FAR], in_sem.at[1]),
        pltpu.make_async_copy(dm_in, dm, in_sem.at[2]),
        pltpu.make_async_copy(w_in, w, in_sem.at[3]),
        pltpu.make_async_copy(q_in, q, in_sem.at[4]),
    ]
    for load in loads:
        load.start()

    barrier = pltpu.get_barrier_semaphore()

    def greet(place):
        pl.semaphore_signal(barrier, 1, device_id={"seq": place}, device_id_type=MESH)

    across = me - 1 + 2 * core
    has_across = (me > 0) & (me < n_seq - 1)
    if levels > 4:
        each(n_seq - 1, lambda i: greet((me + 1 + i) % n_seq))
    else:
        each(n_seq // 2 - 1, lambda i: greet((me + 2 + 2 * i) % n_seq))
        greet(twin)
        pl.when(has_across)(lambda: greet(across))
    pl.semaphore_signal(barrier, 1, device_id={"head": other_head}, device_id_type=MESH)

    @pl.when(me == 0)
    def _():
        kv[:, 0:BLOCK, :] = jnp.zeros((2, BLOCK, feats), BF16)
        hrecv[:, 0:BLOCK, :] = jnp.zeros((2, BLOCK, feats), BF16)

    @pl.when(me == n_seq - 1)
    def _():
        kv[:, BLOCK:HALO, :] = jnp.zeros((2, BLOCK, feats), BF16)
        hrecv[:, BLOCK:HALO, :] = jnp.zeros((2, BLOCK, feats), BF16)

    second = (lax.broadcasted_iota(jnp.int32, (8, 2 * ROWS), 1) // BLOCK) % 2
    missing = ((second == 0) & (me == 0)) | ((second == 1) & (me == n_seq - 1))
    bias[...] = jnp.where(missing, -jnp.inf, 0.0)

    loads[0].wait()
    loads[1].wait()

    spans = []
    for b in range(levels):
        size = 2**b
        span = me // size
        sibling = (span + 1 - 2 * (span % 2)) * size
        mine = me % size
        spans.append((size, BLOCK >> b, sibling, mine))

    k_own = kv[0, HALO:FAR, :]
    v_own = kv[1, HALO:FAR, :]
    for b, (size, rows, sibling, mine) in enumerate(spans):
        if b < 3:
            mat = group_matrix((rows, ROWS), 1, rows, 0)
            psend[b][0] = dot_nn(mat, k_own).astype(BF16)
            psend[b][1] = dot_nn(mat, v_own).astype(BF16)
        else:
            mat = group_matrix((8, ROWS), 1, rows, (mine * rows) % 8)
            psend[b][...] = jnp.concatenate(
                [dot_nn(mat, k_own), dot_nn(mat, v_own)], axis=0
            ).astype(BF16)

    if levels > 4:
        pl.semaphore_wait(barrier, n_seq)
    else:
        greeted = n_seq // 2 + 1
        pl.when(has_across)(lambda: pl.semaphore_wait(barrier, greeted + 1))
        pl.when(jnp.logical_not(has_across))(lambda: pl.semaphore_wait(barrier, greeted))

    def halo_copy(way):
        if way == 0:
            src, dst, to = kv.at[:, HALO + BLOCK : FAR], kv.at[:, 0:BLOCK], me + 1
        else:
            src, dst, to = kv.at[:, HALO : HALO + BLOCK], kv.at[:, BLOCK:HALO], me - 1
        return pltpu.make_async_remote_copy(
            src, dst, halo_s.at[way], halo_r.at[way],
            device_id={"seq": to}, device_id_type=MESH,
        )

    relayed = list(range(1, min(levels, 4)))

    def count(b):
        return 2 ** (b - 1) if b in relayed else 2**b

    def key_rows(b, at, n):
        return kv.at[:, pl.ds(pl.multiple_of(FAR + BLOCK * b + at, 16), n)]

    def far_copy(b, dest, slot):
        size, rows, sibling, mine = spans[b]
        to = sibling + dest
        if b in relayed:
            slot = core * (size // 2) + slot
            to = sibling + 2 * dest + core
        dst = key_rows(b, slot * rows, rows) if b < 3 else srecv[b - 3].at[slot]
        return pltpu.make_async_remote_copy(
            psend[b], dst, far_s.at[size - 1 + dest], far_r.at[size - 1 + slot],
            device_id={"seq": to}, device_id_type=MESH,
        )

    def my_slot(b):
        return mine_of[b] // 2 if b in relayed else mine_of[b]

    mine_of = [span[3] for span in spans]

    def relay_copy(b, part):
        if b < 3:
            ref = key_rows(b, part * (BLOCK // 2), BLOCK // 2)
        else:
            ref = srecv[0].at[pl.ds(part * 4, 4)]
        return pltpu.make_async_remote_copy(
            ref, ref, relay_s.at[b], relay_r.at[b],
            device_id={"seq": twin}, device_id_type=MESH,
        )

    for b in reversed(range(levels)):
        each(count(b), lambda i, b=b: far_copy(b, i, my_slot(b)).start())

    has_next = me < n_seq - 1
    has_prev = me > 0
    pl.when(has_next)(lambda: halo_copy(0).start())
    pl.when(has_prev)(lambda: halo_copy(1).start())

    loads[2].wait()
    loads[3].wait()
    dattn[...] = dot_nt(dm[...], w[...]).astype(BF16)
    loads[4].wait()

    pl.when(has_prev)(lambda: halo_copy(0).wait_recv())
    pl.when(has_next)(lambda: halo_copy(1).wait_recv())
    for b in range(levels):
        each(count(b), lambda i, b=b: far_copy(b, 0, i).wait_recv())
        if b in relayed:
            relay_copy(b, core).start()
    for b in relayed:
        relay_copy(b, 1 - core).wait_recv()

    def place(b, slot):
        return (slot % 2) * 4 + slot // 2 if b == 3 else slot

    for b in range(3, levels):
        rows = spans[b][1]
        per = 8 // rows
        pieces = []
        for g in range(8):
            total = srecv[b - 3][place(b, g * per)].astype(F32)
            for s in range(1, per):
                total = total + srecv[b - 3][g * per + s].astype(F32)
            pieces.append(total)
        at = FAR + BLOCK * b
        for part in range(2):
            kv[part, at : at + BLOCK, :] = jnp.concatenate(
                [piece[8 * part : 8 * part + 8] for piece in pieces], axis=0
            ).astype(BF16)

    lane = lax.broadcasted_iota(jnp.int32, (1, PAIR), 1)
    head_a = jnp.where(lane < HEAD_DIM, 1.0, 0.0).astype(BF16)
    head_b = jnp.where(lane < HEAD_DIM, 0.0, 1.0).astype(BF16)
    token = (lax.broadcasted_iota(jnp.int32, (1, 2 * ROWS), 1) // BLOCK) % 2
    first = token == 0
    mask0 = jnp.where(first, 1.0, 0.0)
    mask1 = jnp.where(first, 0.0, 1.0)

    for pair in range(feats // PAIR):
        cols = slice(pair * PAIR, (pair + 1) * PAIR)
        qp = q[:, cols] * jnp.asarray(0.125, BF16)
        dap = dattn[:, cols]
        qs = jnp.concatenate([qp * head_a, qp * head_b], axis=0)
        das = jnp.concatenate([dap * head_a, dap * head_b], axis=0)
        kp = kv[0, :, cols]
        vp = kv[1, :, cols]

        def merge(full):
            halo = jnp.where(first, full[:BLOCK], full[BLOCK:HALO])
            return halo, full[HALO:]

        s_halo, s_rest = merge(dot_nt(kp, qs))
        s_all = jnp.concatenate([s_halo + bias[0:1, :], s_rest], axis=0)
        top = jnp.max(s_all, axis=0, keepdims=True)
        e_all = jnp.exp(s_all - top)
        normed = e_all * (1.0 / jnp.sum(e_all, axis=0, keepdims=True))

        def unmerge(full):
            halo = full[:BLOCK]
            return jnp.concatenate(
                [halo * mask0, halo * mask1, full[BLOCK:]], axis=0
            ).astype(BF16)

        weights = unmerge(normed)
        d_halo, d_rest = merge(dot_nt(vp, das))
        d_normed = jnp.concatenate([d_halo, d_rest], axis=0)
        inner = jnp.sum(normed * d_normed, axis=0, keepdims=True)
        d_scores = unmerge(normed * (d_normed - inner))

        def both(values_t, coeffs):
            full = dot_nn(values_t, coeffs)
            return jnp.concatenate(
                [full[:HEAD_DIM, :ROWS], full[HEAD_DIM:, ROWS:]], axis=0
            ).T

        attn[:, cols] = both(vp.T, weights).astype(BF16)
        dq[:, cols] = (both(kp.T, d_scores) * 0.125).astype(BF16)
        grads = (dot_nn(d_scores, qs), dot_nn(weights, das))
        for part in range(2):
            grad = grads[part]
            hsend[part, :, cols] = grad[:HALO].astype(BF16)
            gown[part, :, cols] = grad[HALO:FAR]
            gsend[part, :, cols] = grad[FAR : FAR + BLOCK * big].astype(BF16)
        for b in range(3, levels):
            at = FAR + BLOCK * b
            for g in range(8):
                gssend[b - 3][place(b, g), :, cols] = jnp.concatenate(
                    [grad[at + 8 * g : at + 8 * g + 8] for grad in grads], axis=0
                ).astype(BF16)

    def ghalo_copy(way):
        if way == 0:
            src, dst, to = hsend.at[:, 0:BLOCK], hrecv.at[:, BLOCK:HALO], me - 1
        else:
            src, dst, to = hsend.at[:, BLOCK:HALO], hrecv.at[:, 0:BLOCK], me + 1
        return pltpu.make_async_remote_copy(
            src, dst, ghalo_s.at[way], ghalo_r.at[way],
            device_id={"seq": to}, device_id_type=MESH,
        )

    def sum_copy(b):
        half = BLOCK // 2
        if b < 3:
            at = BLOCK * b + (1 - core) * half
            src = gsend.at[:, pl.ds(pl.multiple_of(at, half), half)]
            dst = sum_recv.at[:, half * (b - 1) : half * b]
        else:
            src = gssend[0].at[pl.ds((1 - core) * 4, 4)]
            dst = small_recv
        return pltpu.make_async_remote_copy(
            src, dst, sum_s.at[b], sum_r.at[b],
            device_id={"seq": twin}, device_id_type=MESH,
        )

    def gfar_copy(b, dest, slot):
        size, rows, sibling, mine = spans[b]
        to = sibling + dest
        if b == 0:
            src, dst = gsend.at[:, 0:BLOCK], grecv.at[:, 0:BLOCK]
        elif b < 3:
            half = BLOCK // 2
            src = sum_send.at[:, pl.ds(pl.multiple_of(half * (b - 1) + dest * rows, 16), rows)]
            dst = grecv.at[:, pl.ds(pl.multiple_of(half * (b + 1) + slot * rows, 16), rows)]
        elif b == 3:
            src, dst = small_send.at[dest], gsrecv[0].at[slot]
        else:
            src = gssend[b - 3].at[dest // (8 // rows)]
            dst = gsrecv[b - 3].at[slot]
        if b in relayed:
            to = sibling + 2 * dest + core
        return pltpu.make_async_remote_copy(
            src, dst, gfar_s.at[size - 1 + dest], gfar_r.at[size - 1 + slot],
            device_id={"seq": to}, device_id_type=MESH,
        )

    for b in reversed(relayed):
        sum_copy(b).start()
    pl.when(has_prev)(lambda: ghalo_copy(0).start())
    pl.when(has_next)(lambda: ghalo_copy(1).start())
    for b in reversed(range(levels)):
        if b in relayed:
            sum_copy(b).wait_recv()
            half = BLOCK // 2
            if b < 3:
                mine_rows = pl.ds(pl.multiple_of(BLOCK * b + core * half, half), half)
                own = gsend[:, mine_rows, :].astype(F32)
                both_cores = own + sum_recv[:, half * (b - 1) : half * b, :].astype(F32)
                sum_send[:, half * (b - 1) : half * b, :] = both_cores.astype(BF16)
            else:
                own = gssend[0][pl.ds(core * 4, 4)].astype(F32)
                small_send[...] = (own + small_recv[...].astype(F32)).astype(BF16)
        each(count(b), lambda i, b=b: gfar_copy(b, i, my_slot(b)).start())

    theirs = pl.ds(pl.multiple_of(other_head * BLOCK, BLOCK), BLOCK)
    ours = pl.ds(pl.multiple_of(hd * BLOCK, BLOCK), BLOCK)
    mix_send[...] = dot_nn(attn[theirs, :], w[...]).astype(BF16)
    mix_copy = pltpu.make_async_remote_copy(
        mix_send, mix_recv, mix_sem.at[0], mix_sem.at[1],
        device_id={"head": other_head}, device_id_type=MESH,
    )
    mix_copy.start()
    mix_own[...] = dot_nn(attn[ours, :], w[...])

    pl.when(has_next)(lambda: ghalo_copy(0).wait_recv())
    pl.when(has_prev)(lambda: ghalo_copy(1).wait_recv())
    for b in range(levels):
        each(count(b), lambda i, b=b: gfar_copy(b, 0, i).wait_recv())

    for part in range(2):
        total = gown[part] + hrecv[part].astype(F32)
        for b, (size, rows, sibling, mine) in enumerate(spans):
            if b < 3:
                wide = rows * count(b)
                at = BLOCK // 2 * (b + 1) if b else 0
                token = lax.broadcasted_iota(jnp.int32, (ROWS, wide), 0)
                row = lax.broadcasted_iota(jnp.int32, (ROWS, wide), 1)
                group = ROWS // rows
                mat = jnp.where(token // group == row % rows, 1.0 / group, 0.0).astype(BF16)
                total = total + dot_nn(mat, grecv[part, at : at + wide, :])
            else:
                wide = 16 * count(b)
                token = lax.broadcasted_iota(jnp.int32, (ROWS, wide), 0)
                row = lax.broadcasted_iota(jnp.int32, (ROWS, wide), 1) % 16
                group = ROWS // rows
                wanted = token // group + (mine * rows) % 8 + 8 * part
                mat = jnp.where(wanted == row, 1.0 / group, 0.0).astype(BF16)
                total = total + dot_nn(mat, gsrecv[b - 3][...].reshape(wide, feats))
        (dk_out, dv_out)[part][...] = total.astype(BF16)

    mix_copy.wait_recv()
    mixed_out[...] = (mix_own[...] + mix_recv[...].astype(F32)).astype(BF16)

    pl.when(has_next)(lambda: halo_copy(0).wait_send())
    pl.when(has_prev)(lambda: halo_copy(1).wait_send())
    pl.when(has_prev)(lambda: ghalo_copy(0).wait_send())
    pl.when(has_next)(lambda: ghalo_copy(1).wait_send())
    for b in range(levels):
        each(count(b), lambda i, b=b: far_copy(b, i, my_slot(b)).wait_send())
        each(count(b), lambda i, b=b: gfar_copy(b, i, my_slot(b)).wait_send())
    for b in relayed:
        relay_copy(b, core).wait_send()
        sum_copy(b).wait_send()
    mix_copy.wait_send()


def write_kernel(*refs):
    for i in range(4):
        refs[4 + i][...] = refs[i][...]


def on_device(n_seq, queries, keys, values, w_out, d_mixed):
    feats = queries.shape[1]
    width = w_out.shape[1]
    levels = n_seq.bit_length() - 1
    big = min(levels, 3)
    small = list(range(3, levels))
    n_keys = FAR + BLOCK * levels
    vmem = pltpu.VMEM
    dma = pltpu.SemaphoreType.DMA
    scratch = [
        vmem((ROWS, feats), BF16),
        vmem((feats, width), BF16),
        vmem((ROWS, width), BF16),
        vmem((2, n_keys, feats), BF16),
        vmem((ROWS, feats), BF16),
        vmem((ROWS, feats), BF16),
        vmem((8, 2 * ROWS), F32),
        vmem((2, ROWS, feats), F32),
        vmem((2, HALO, feats), BF16),
        vmem((2, HALO, feats), BF16),
        vmem((2, BLOCK * big, feats), BF16),
        vmem((2, 2 * BLOCK, feats), BF16),
        vmem((BLOCK, width), BF16),
        vmem((BLOCK, width), BF16),
        vmem((BLOCK, width), F32),
        dma((5,)),
        dma((2,)),
        dma((2,)),
        dma((n_seq - 1,)),
        dma((n_seq - 1,)),
        dma((2,)),
        dma((2,)),
        dma((n_seq - 1,)),
        dma((n_seq - 1,)),
        dma((2,)),
        dma((4,)),
        dma((4,)),
        dma((4,)),
        dma((4,)),
        vmem((2, BLOCK, feats), BF16),
        vmem((2, BLOCK, feats), BF16),
        vmem((4, 16, feats), BF16),
        vmem((4, 16, feats), BF16),
    ]
    scratch += [vmem((2, BLOCK >> b, feats), BF16) for b in range(big)]
    scratch += [vmem((16, feats), BF16) for b in small]
    scratch += [vmem((2**b, 16, feats), BF16) for b in small]
    scratch += [vmem((8, 16, feats), BF16) for b in small]
    scratch += [vmem((2**b // (2 if b == 3 else 1), 16, feats), BF16) for b in small]
    in_hbm = pl.BlockSpec(memory_space=pltpu.HBM)
    in_vmem = pl.BlockSpec(memory_space=pltpu.VMEM)
    shapes = [
        jax.ShapeDtypeStruct((BLOCK, width), BF16),
        jax.ShapeDtypeStruct((ROWS, feats), BF16),
        jax.ShapeDtypeStruct((ROWS, feats), BF16),
        jax.ShapeDtypeStruct((ROWS, feats), BF16),
    ]
    results = pl.pallas_call(
        functools.partial(kernel, n_seq, levels),
        out_shape=shapes,
        in_specs=[in_hbm] * 5,
        out_specs=[in_vmem] * 4,
        scratch_shapes=scratch,
        compiler_params=pltpu.CompilerParams(
            collective_id=0, has_side_effects=True, vmem_limit_bytes=63 * 2**20
        ),
    )(queries, keys, values, w_out, d_mixed)
    return pl.pallas_call(
        write_kernel,
        out_shape=shapes,
        in_specs=[in_vmem] * 4,
        out_specs=[in_vmem] * 4,
        compiler_params=pltpu.CompilerParams(vmem_limit_bytes=63 * 2**20),
    )(*results)


def solution(mesh):
    in_specs = (
        P("seq", "head"),
        P("seq", "head"),
        P("seq", "head"),
        P("head", None),
        P("seq", None),
    )
    out_specs = (P(("seq", "head"), None), P("seq", "head"), P("seq", "head"), P("seq", "head"))
    return jax.shard_map(
        functools.partial(on_device, mesh.shape["seq"]),
        mesh=mesh,
        in_specs=in_specs,
        out_specs=out_specs,
        check_vma=False,
    )
```

```python
import functools

import jax
import jax.numpy as jnp
from jax import lax
from jax.experimental import pallas as pl
from jax.experimental.pallas import tpu as pltpu
from jax.sharding import PartitionSpec as P

HEAD_DIM = 64
BLOCK = 64
ROWS = 128
PAIR = 2 * HEAD_DIM
HALO = 2 * BLOCK
FAR = HALO + ROWS
MESH = pl.DeviceIdType.MESH
BF16 = jnp.bfloat16
F32 = jnp.float32


def dot_nt(left, right):
    return lax.dot_general(
        left, right, (((1,), (1,)), ((), ())), preferred_element_type=F32
    )


def dot_nn(left, right):
    return jnp.dot(left, right, preferred_element_type=F32)


def each(count, step):
    if count <= 8:
        for i in range(count):
            step(i)
    else:
        lax.fori_loop(0, count, lambda i, c: (step(i), c)[1], 0)


def group_matrix(shape, token_dim, rows, first):
    group = ROWS // rows
    token = lax.broadcasted_iota(jnp.int32, shape, token_dim)
    other = lax.broadcasted_iota(jnp.int32, shape, 1 - token_dim)
    return jnp.where(token // group + first == other, 1.0 / group, 0.0).astype(BF16)


def kernel(n_seq, levels, *refs):
    q_in, k_in, v_in, w_in, dm_in, mixed_out, dq, dk_out, dv_out = refs[:9]
    (
        q, w, dm, kv, dattn, attn, bias, gown, hsend, hrecv, gsend, grecv,
        mix_send, mix_recv, mix_own,
        in_sem, halo_s, halo_r, far_s, far_r,
        ghalo_s, ghalo_r, gfar_s, gfar_r, mix_sem,
        relay_s, relay_r, sum_s, sum_r, sum_recv, sum_send, small_recv, small_send,
    ) = refs[9:42]
    rest = refs[42:]
    psend = rest[:levels]
    n_small = max(levels - 3, 0)
    srecv = rest[levels : levels + n_small]
    gssend = rest[levels + n_small : levels + 2 * n_small]
    gsrecv = rest[levels + 2 * n_small :]
    feats = q.shape[1]
    big = min(levels, 3)
    me = lax.axis_index("seq")
    hd = lax.axis_index("head")
    other_head = 1 - hd
    core = me % 2
    part_of = (slice(0, feats // 2), slice(feats // 2, feats))
    twin = me + 1 - 2 * core

    loads = [
        pltpu.make_async_copy(k_in, kv.at[0, HALO:FAR], in_sem.at[0]),
        pltpu.make_async_copy(v_in, kv.at[1, HALO:FAR], in_sem.at[1]),
        pltpu.make_async_copy(dm_in, dm, in_sem.at[2]),
        pltpu.make_async_copy(w_in, w, in_sem.at[3]),
        pltpu.make_async_copy(q_in, q, in_sem.at[4]),
    ]
    for load in loads:
        load.start()

    barrier = pltpu.get_barrier_semaphore()

    def greet(place):
        pl.semaphore_signal(barrier, 1, device_id={"seq": place}, device_id_type=MESH)

    across = me - 1 + 2 * core
    has_across = (me > 0) & (me < n_seq - 1)
    if levels > 4:
        each(n_seq - 1, lambda i: greet((me + 1 + i) % n_seq))
    else:
        each(n_seq // 2 - 1, lambda i: greet((me + 2 + 2 * i) % n_seq))
        greet(twin)
        pl.when(has_across)(lambda: greet(across))
    pl.semaphore_signal(barrier, 1, device_id={"head": other_head}, device_id_type=MESH)

    @pl.when(me == 0)
    def _():
        kv[:, 0:BLOCK, :] = jnp.zeros((2, BLOCK, feats), BF16)
        hrecv[:, 0:BLOCK, :] = jnp.zeros((2, BLOCK, feats), BF16)

    @pl.when(me == n_seq - 1)
    def _():
        kv[:, BLOCK:HALO, :] = jnp.zeros((2, BLOCK, feats), BF16)
        hrecv[:, BLOCK:HALO, :] = jnp.zeros((2, BLOCK, feats), BF16)

    second = (lax.broadcasted_iota(jnp.int32, (8, 2 * ROWS), 1) // BLOCK) % 2
    missing = ((second == 0) & (me == 0)) | ((second == 1) & (me == n_seq - 1))
    bias[...] = jnp.where(missing, -jnp.inf, 0.0)

    loads[0].wait()
    loads[1].wait()

    spans = []
    for b in range(levels):
        size = 2**b
        span = me // size
        sibling = (span + 1 - 2 * (span % 2)) * size
        mine = me % size
        spans.append((size, BLOCK >> b, sibling, mine))

    k_own = kv[0, HALO:FAR, :]
    v_own = kv[1, HALO:FAR, :]
    for b, (size, rows, sibling, mine) in enumerate(spans):
        if b < 3:
            mat = group_matrix((rows, ROWS), 1, rows, 0)
            psend[b][0] = dot_nn(mat, k_own).astype(BF16)
            psend[b][1] = dot_nn(mat, v_own).astype(BF16)
        else:
            mat = group_matrix((8, ROWS), 1, rows, (mine * rows) % 8)
            psend[b][...] = jnp.concatenate(
                [dot_nn(mat, k_own), dot_nn(mat, v_own)], axis=0
            ).astype(BF16)

    if levels > 4:
        pl.semaphore_wait(barrier, n_seq)
    else:
        greeted = n_seq // 2 + 1
        pl.when(has_across)(lambda: pl.semaphore_wait(barrier, greeted + 1))
        pl.when(jnp.logical_not(has_across))(lambda: pl.semaphore_wait(barrier, greeted))

    def halo_copy(way, h):
        if way == 0:
            src, dst, to = kv.at[:, HALO + BLOCK : FAR, part_of[h]], kv.at[:, 0:BLOCK, part_of[h]], me + 1
        else:
            src, dst, to = kv.at[:, HALO : HALO + BLOCK, part_of[h]], kv.at[:, BLOCK:HALO, part_of[h]], me - 1
        return pltpu.make_async_remote_copy(
            src, dst, halo_s.at[h, way], halo_r.at[h, way],
            device_id={"seq": to}, device_id_type=MESH,
        )

    relayed = list(range(1, min(levels, 4)))

    def count(b):
        return 2 ** (b - 1) if b in relayed else 2**b

    def key_rows(b, at, n, h):
        return kv.at[:, pl.ds(pl.multiple_of(FAR + BLOCK * b + at, 16), n), part_of[h]]

    def far_copy(b, dest, slot, h):
        size, rows, sibling, mine = spans[b]
        to = sibling + dest
        if b in relayed:
            slot = core * (size // 2) + slot
            to = sibling + 2 * dest + core
        if b < 3:
            src, dst = psend[b].at[:, :, part_of[h]], key_rows(b, slot * rows, rows, h)
        else:
            src, dst = psend[b].at[:, part_of[h]], srecv[b - 3].at[slot, :, part_of[h]]
        return pltpu.make_async_remote_copy(
            src, dst, far_s.at[h, size - 1 + dest], far_r.at[h, size - 1 + slot],
            device_id={"seq": to}, device_id_type=MESH,
        )

    def my_slot(b):
        return mine_of[b] // 2 if b in relayed else mine_of[b]

    mine_of = [span[3] for span in spans]

    def relay_copy(b, part, h):
        if b < 3:
            ref = key_rows(b, part * (BLOCK // 2), BLOCK // 2, h)
        else:
            ref = srecv[0].at[pl.ds(part * 4, 4), :, part_of[h]]
        return pltpu.make_async_remote_copy(
            ref, ref, relay_s.at[h, b], relay_r.at[h, b],
            device_id={"seq": twin}, device_id_type=MESH,
        )

    has_next = me < n_seq - 1
    has_prev = me > 0
    for h in range(2):
        for b in reversed(range(levels)):
            each(count(b), lambda i: far_copy(b, i, my_slot(b), h).start())
        pl.when(has_next)(lambda: halo_copy(0, h).start())
        pl.when(has_prev)(lambda: halo_copy(1, h).start())

    loads[2].wait()
    loads[3].wait()
    dattn[...] = dot_nt(dm[...], w[...]).astype(BF16)
    loads[4].wait()

    def hand_on(h):
        for b in reversed(relayed):
            each(count(b), lambda i: far_copy(b, 0, i, h).wait_recv())
            relay_copy(b, core, h).start()

    def place(b, slot):
        return (slot % 2) * 4 + slot // 2 if b == 3 else slot

    def collect(h):
        pl.when(has_prev)(lambda: halo_copy(0, h).wait_recv())
        pl.when(has_next)(lambda: halo_copy(1, h).wait_recv())
        for b in range(levels):
            if b in relayed:
                relay_copy(b, 1 - core, h).wait_recv()
            else:
                each(count(b), lambda i: far_copy(b, 0, i, h).wait_recv())
        for b in range(3, levels):
            per = 8 // spans[b][1]
            pieces = []
            for g in range(8):
                total = srecv[b - 3][place(b, g * per), :, part_of[h]].astype(F32)
                for s in range(1, per):
                    total = total + srecv[b - 3][g * per + s, :, part_of[h]].astype(F32)
                pieces.append(total)
            at = FAR + BLOCK * b
            for part in range(2):
                kv[part, at : at + BLOCK, part_of[h]] = jnp.concatenate(
                    [piece[8 * part : 8 * part + 8] for piece in pieces], axis=0
                ).astype(BF16)

    lane = lax.broadcasted_iota(jnp.int32, (1, PAIR), 1)
    head_a = jnp.where(lane < HEAD_DIM, 1.0, 0.0).astype(BF16)
    head_b = jnp.where(lane < HEAD_DIM, 0.0, 1.0).astype(BF16)
    token = (lax.broadcasted_iota(jnp.int32, (1, 2 * ROWS), 1) // BLOCK) % 2
    first = token == 0
    mask0 = jnp.where(first, 1.0, 0.0)
    mask1 = jnp.where(first, 0.0, 1.0)

    def attend(pair):
        cols = slice(pair * PAIR, (pair + 1) * PAIR)
        qp = q[:, cols] * jnp.asarray(0.125, BF16)
        dap = dattn[:, cols]
        qs = jnp.concatenate([qp * head_a, qp * head_b], axis=0)
        das = jnp.concatenate([dap * head_a, dap * head_b], axis=0)
        kp = kv[0, :, cols]
        vp = kv[1, :, cols]

        def merge(full):
            halo = jnp.where(first, full[:BLOCK], full[BLOCK:HALO])
            return halo, full[HALO:]

        s_halo, s_rest = merge(dot_nt(kp, qs))
        s_all = jnp.concatenate([s_halo + bias[0:1, :], s_rest], axis=0)
        top = jnp.max(s_all, axis=0, keepdims=True)
        e_all = jnp.exp(s_all - top)
        normed = e_all * (1.0 / jnp.sum(e_all, axis=0, keepdims=True))

        def unmerge(full):
            halo = full[:BLOCK]
            return jnp.concatenate(
                [halo * mask0, halo * mask1, full[BLOCK:]], axis=0
            ).astype(BF16)

        weights = unmerge(normed)
        d_halo, d_rest = merge(dot_nt(vp, das))
        d_normed = jnp.concatenate([d_halo, d_rest], axis=0)
        inner = jnp.sum(normed * d_normed, axis=0, keepdims=True)
        d_scores = unmerge(normed * (d_normed - inner))

        def both(values_t, coeffs):
            full = dot_nn(values_t, coeffs)
            return jnp.concatenate(
                [full[:HEAD_DIM, :ROWS], full[HEAD_DIM:, ROWS:]], axis=0
            ).T

        attn[:, cols] = both(vp.T, weights).astype(BF16)
        dq[:, cols] = (both(kp.T, d_scores) * 0.125).astype(BF16)
        grads = (dot_nn(d_scores, qs), dot_nn(weights, das))
        for part in range(2):
            grad = grads[part]
            hsend[part, :, cols] = grad[:HALO].astype(BF16)
            gown[part, :, cols] = grad[HALO:FAR]
            gsend[part, :, cols] = grad[FAR : FAR + BLOCK * big].astype(BF16)
        for b in range(3, levels):
            at = FAR + BLOCK * b
            for g in range(8):
                gssend[b - 3][place(b, g), :, cols] = jnp.concatenate(
                    [grad[at + 8 * g : at + 8 * g + 8] for grad in grads], axis=0
                ).astype(BF16)

    def ghalo_copy(way, h):
        if way == 0:
            src, dst, to = hsend.at[:, 0:BLOCK, part_of[h]], hrecv.at[:, BLOCK:HALO, part_of[h]], me - 1
        else:
            src, dst, to = hsend.at[:, BLOCK:HALO, part_of[h]], hrecv.at[:, 0:BLOCK, part_of[h]], me + 1
        return pltpu.make_async_remote_copy(
            src, dst, ghalo_s.at[h, way], ghalo_r.at[h, way],
            device_id={"seq": to}, device_id_type=MESH,
        )

    def sum_copy(b, h):
        half = BLOCK // 2
        if b < 3:
            at = BLOCK * b + (1 - core) * half
            src = gsend.at[:, pl.ds(pl.multiple_of(at, half), half), part_of[h]]
            dst = sum_recv.at[:, half * (b - 1) : half * b, part_of[h]]
        else:
            src = gssend[0].at[pl.ds((1 - core) * 4, 4), :, part_of[h]]
            dst = small_recv.at[:, :, part_of[h]]
        return pltpu.make_async_remote_copy(
            src, dst, sum_s.at[h, b], sum_r.at[h, b],
            device_id={"seq": twin}, device_id_type=MESH,
        )

    def gfar_copy(b, dest, slot, h):
        size, rows, sibling, mine = spans[b]
        to = sibling + dest
        if b == 0:
            src, dst = gsend.at[:, 0:BLOCK, part_of[h]], grecv.at[:, 0:BLOCK, part_of[h]]
        elif b < 3:
            half = BLOCK // 2
            src = sum_send.at[:, pl.ds(pl.multiple_of(half * (b - 1) + dest * rows, 16), rows), part_of[h]]
            dst = grecv.at[:, pl.ds(pl.multiple_of(half * (b + 1) + slot * rows, 16), rows), part_of[h]]
        elif b == 3:
            src, dst = small_send.at[dest, :, part_of[h]], gsrecv[0].at[slot, :, part_of[h]]
        else:
            src = gssend[b - 3].at[dest // (8 // rows), :, part_of[h]]
            dst = gsrecv[b - 3].at[slot, :, part_of[h]]
        if b in relayed:
            to = sibling + 2 * dest + core
        return pltpu.make_async_remote_copy(
            src, dst, gfar_s.at[h, size - 1 + dest], gfar_r.at[h, size - 1 + slot],
            device_id={"seq": to}, device_id_type=MESH,
        )

    def give_back(h):
        for b in reversed(relayed):
            sum_copy(b, h).start()
        pl.when(has_prev)(lambda: ghalo_copy(0, h).start())
        pl.when(has_next)(lambda: ghalo_copy(1, h).start())
        for b in range(levels):
            if b not in relayed:
                each(count(b), lambda i: gfar_copy(b, i, my_slot(b), h).start())

    def give_back_sums(h):
        half = BLOCK // 2
        for b in reversed(relayed):
            sum_copy(b, h).wait_recv()
            if b < 3:
                mine_rows = pl.ds(pl.multiple_of(BLOCK * b + core * half, half), half)
                own = gsend[:, mine_rows, part_of[h]].astype(F32)
                theirs = sum_recv[:, half * (b - 1) : half * b, part_of[h]].astype(F32)
                sum_send[:, half * (b - 1) : half * b, part_of[h]] = (own + theirs).astype(BF16)
            else:
                own = gssend[0][pl.ds(core * 4, 4), :, part_of[h]].astype(F32)
                theirs = small_recv[:, :, part_of[h]].astype(F32)
                small_send[:, :, part_of[h]] = (own + theirs).astype(BF16)
            each(count(b), lambda i: gfar_copy(b, i, my_slot(b), h).start())

    pairs = feats // PAIR // 2
    hand_on(0)
    collect(0)
    for pair in range(pairs):
        attend(pair)
        if pair == 0:
            hand_on(1)
    give_back(0)
    collect(1)
    for pair in range(pairs, 2 * pairs):
        attend(pair)
        if pair == pairs:
            give_back_sums(0)
    give_back(1)

    theirs = pl.ds(pl.multiple_of(other_head * BLOCK, BLOCK), BLOCK)
    ours = pl.ds(pl.multiple_of(hd * BLOCK, BLOCK), BLOCK)
    mix_send[...] = dot_nn(attn[theirs, :], w[...]).astype(BF16)
    mix_copy = pltpu.make_async_remote_copy(
        mix_send, mix_recv, mix_sem.at[0], mix_sem.at[1],
        device_id={"head": other_head}, device_id_type=MESH,
    )
    mix_copy.start()
    give_back_sums(1)
    mix_own[...] = dot_nn(attn[ours, :], w[...])

    for h in range(2):
        pl.when(has_next)(lambda: ghalo_copy(0, h).wait_recv())
        pl.when(has_prev)(lambda: ghalo_copy(1, h).wait_recv())
        for b in range(levels):
            each(count(b), lambda i: gfar_copy(b, 0, i, h).wait_recv())
        for part in range(2):
            total = gown[part, :, part_of[h]] + hrecv[part, :, part_of[h]].astype(F32)
            for b, (size, rows, sibling, mine) in enumerate(spans):
                group = ROWS // rows
                wide = (rows if b < 3 else 16) * count(b)
                token = lax.broadcasted_iota(jnp.int32, (ROWS, wide), 0)
                row = lax.broadcasted_iota(jnp.int32, (ROWS, wide), 1)
                if b < 3:
                    at = BLOCK // 2 * (b + 1) if b else 0
                    same = token // group == row % rows
                    got = grecv[part, at : at + wide, part_of[h]]
                else:
                    same = token // group + (mine * rows) % 8 + 8 * part == row % 16
                    got = gsrecv[b - 3][:, :, part_of[h]].reshape(wide, feats // 2)
                mat = jnp.where(same, 1.0 / group, 0.0).astype(BF16)
                total = total + dot_nn(mat, got)
            (dk_out, dv_out)[part][:, part_of[h]] = total.astype(BF16)

    mix_copy.wait_recv()
    mixed_out[...] = (mix_own[...] + mix_recv[...].astype(F32)).astype(BF16)

    for h in range(2):
        pl.when(has_next)(lambda: halo_copy(0, h).wait_send())
        pl.when(has_prev)(lambda: halo_copy(1, h).wait_send())
        pl.when(has_prev)(lambda: ghalo_copy(0, h).wait_send())
        pl.when(has_next)(lambda: ghalo_copy(1, h).wait_send())
        for b in range(levels):
            each(count(b), lambda i: far_copy(b, i, my_slot(b), h).wait_send())
            each(count(b), lambda i: gfar_copy(b, i, my_slot(b), h).wait_send())
        for b in relayed:
            relay_copy(b, core, h).wait_send()
            sum_copy(b, h).wait_send()
    mix_copy.wait_send()


def write_kernel(*refs):
    for i in range(4):
        refs[4 + i][...] = refs[i][...]


def on_device(n_seq, queries, keys, values, w_out, d_mixed):
    feats = queries.shape[1]
    width = w_out.shape[1]
    levels = n_seq.bit_length() - 1
    big = min(levels, 3)
    small = list(range(3, levels))
    n_keys = FAR + BLOCK * levels
    vmem = pltpu.VMEM
    dma = pltpu.SemaphoreType.DMA
    scratch = [
        vmem((ROWS, feats), BF16),
        vmem((feats, width), BF16),
        vmem((ROWS, width), BF16),
        vmem((2, n_keys, feats), BF16),
        vmem((ROWS, feats), BF16),
        vmem((ROWS, feats), BF16),
        vmem((8, 2 * ROWS), F32),
        vmem((2, ROWS, feats), F32),
        vmem((2, HALO, feats), BF16),
        vmem((2, HALO, feats), BF16),
        vmem((2, BLOCK * big, feats), BF16),
        vmem((2, 2 * BLOCK, feats), BF16),
        vmem((BLOCK, width), BF16),
        vmem((BLOCK, width), BF16),
        vmem((BLOCK, width), F32),
        dma((5,)),
        dma((2, 2)),
        dma((2, 2)),
        dma((2, n_seq - 1)),
        dma((2, n_seq - 1)),
        dma((2, 2)),
        dma((2, 2)),
        dma((2, n_seq - 1)),
        dma((2, n_seq - 1)),
        dma((2,)),
        dma((2, 4)),
        dma((2, 4)),
        dma((2, 4)),
        dma((2, 4)),
        vmem((2, BLOCK, feats), BF16),
        vmem((2, BLOCK, feats), BF16),
        vmem((4, 16, feats), BF16),
        vmem((4, 16, feats), BF16),
    ]
    scratch += [vmem((2, BLOCK >> b, feats), BF16) for b in range(big)]
    scratch += [vmem((16, feats), BF16) for b in small]
    scratch += [vmem((2**b, 16, feats), BF16) for b in small]
    scratch += [vmem((8, 16, feats), BF16) for b in small]
    scratch += [vmem((2**b // (2 if b == 3 else 1), 16, feats), BF16) for b in small]
    in_hbm = pl.BlockSpec(memory_space=pltpu.HBM)
    in_vmem = pl.BlockSpec(memory_space=pltpu.VMEM)
    shapes = [
        jax.ShapeDtypeStruct((BLOCK, width), BF16),
        jax.ShapeDtypeStruct((ROWS, feats), BF16),
        jax.ShapeDtypeStruct((ROWS, feats), BF16),
        jax.ShapeDtypeStruct((ROWS, feats), BF16),
    ]
    results = pl.pallas_call(
        functools.partial(kernel, n_seq, levels),
        out_shape=shapes,
        in_specs=[in_hbm] * 5,
        out_specs=[in_vmem] * 4,
        scratch_shapes=scratch,
        compiler_params=pltpu.CompilerParams(
            collective_id=0, has_side_effects=True, vmem_limit_bytes=63 * 2**20
        ),
    )(queries, keys, values, w_out, d_mixed)
    return pl.pallas_call(
        write_kernel,
        out_shape=shapes,
        in_specs=[in_vmem] * 4,
        out_specs=[in_vmem] * 4,
        compiler_params=pltpu.CompilerParams(vmem_limit_bytes=63 * 2**20),
    )(*results)


def solution(mesh):
    in_specs = (
        P("seq", "head"),
        P("seq", "head"),
        P("seq", "head"),
        P("head", None),
        P("seq", None),
    )
    out_specs = (P(("seq", "head"), None), P("seq", "head"), P("seq", "head"), P("seq", "head"))
    return jax.shard_map(
        functools.partial(on_device, mesh.shape["seq"]),
        mesh=mesh,
        in_specs=in_specs,
        out_specs=out_specs,
        check_vma=False,
    )
```

```python
import functools

import jax
import jax.numpy as jnp
from jax import lax
from jax.experimental import pallas as pl
from jax.experimental.pallas import tpu as pltpu
from jax.sharding import PartitionSpec as P

HEAD_DIM = 64
BLOCK = 64
ROWS = 128
PAIR = 2 * HEAD_DIM
HALO = 2 * BLOCK
FAR = HALO + ROWS
MESH = pl.DeviceIdType.MESH
BF16 = jnp.bfloat16
F32 = jnp.float32


def dot_nt(left, right):
    return lax.dot_general(
        left, right, (((1,), (1,)), ((), ())), preferred_element_type=F32
    )


def dot_nn(left, right):
    return jnp.dot(left, right, preferred_element_type=F32)


def each(count, step):
    if count <= 8:
        for i in range(count):
            step(i)
    else:
        lax.fori_loop(0, count, lambda i, c: (step(i), c)[1], 0)


def group_matrix(shape, token_dim, rows, first):
    group = ROWS // rows
    token = lax.broadcasted_iota(jnp.int32, shape, token_dim)
    other = lax.broadcasted_iota(jnp.int32, shape, 1 - token_dim)
    return jnp.where(token // group + first == other, 1.0 / group, 0.0).astype(BF16)


def kernel(n_seq, levels, *refs):
    q_in, k_in, v_in, w_in, dm_in, mixed_out, dq, dk_out, dv_out = refs[:9]
    (
        q, w, dm, kv, dattn, attn, bias, gown, hsend, hrecv, gsend, grecv,
        mix_send, mix_recv, mix_own,
        in_sem, halo_s, halo_r, far_s, far_r,
        ghalo_s, ghalo_r, gfar_s, gfar_r, mix_sem,
        relay_s, relay_r, sum_s, sum_r, sum_recv, sum_send, small_recv, small_send,
    ) = refs[9:42]
    rest = refs[42:]
    psend = rest[:levels]
    n_small = max(levels - 3, 0)
    srecv = rest[levels : levels + n_small]
    gssend = rest[levels + n_small : levels + 2 * n_small]
    gsrecv = rest[levels + 2 * n_small :]
    feats = q.shape[1]
    big = min(levels, 3)
    me = lax.axis_index("seq")
    hd = lax.axis_index("head")
    other_head = 1 - hd
    core = me % 2
    part_of = (slice(0, feats // 2), slice(feats // 2, feats))
    twin = me + 1 - 2 * core

    loads = [
        pltpu.make_async_copy(k_in, kv.at[0, HALO:FAR], in_sem.at[0]),
        pltpu.make_async_copy(v_in, kv.at[1, HALO:FAR], in_sem.at[1]),
        pltpu.make_async_copy(dm_in, dm, in_sem.at[2]),
        pltpu.make_async_copy(w_in, w, in_sem.at[3]),
        pltpu.make_async_copy(q_in, q, in_sem.at[4]),
    ]
    for load in loads:
        load.start()

    barrier = pltpu.get_barrier_semaphore()

    def greet(place):
        pl.semaphore_signal(barrier, 1, device_id={"seq": place}, device_id_type=MESH)

    across = me - 1 + 2 * core
    has_across = (me > 0) & (me < n_seq - 1)
    if levels > 4:
        each(n_seq - 1, lambda i: greet((me + 1 + i) % n_seq))
    else:
        each(n_seq // 2 - 1, lambda i: greet((me + 2 + 2 * i) % n_seq))
        greet(twin)
        pl.when(has_across)(lambda: greet(across))
    pl.semaphore_signal(barrier, 1, device_id={"head": other_head}, device_id_type=MESH)

    @pl.when(me == 0)
    def _():
        kv[:, 0:BLOCK, :] = jnp.zeros((2, BLOCK, feats), BF16)
        hrecv[:, 0:BLOCK, :] = jnp.zeros((2, BLOCK, feats), BF16)

    @pl.when(me == n_seq - 1)
    def _():
        kv[:, BLOCK:HALO, :] = jnp.zeros((2, BLOCK, feats), BF16)
        hrecv[:, BLOCK:HALO, :] = jnp.zeros((2, BLOCK, feats), BF16)

    second = (lax.broadcasted_iota(jnp.int32, (8, 2 * ROWS), 1) // BLOCK) % 2
    missing = ((second == 0) & (me == 0)) | ((second == 1) & (me == n_seq - 1))
    bias[...] = jnp.where(missing, -jnp.inf, 0.0)

    loads[0].wait()
    loads[1].wait()

    spans = []
    for b in range(levels):
        size = 2**b
        span = me // size
        sibling = (span + 1 - 2 * (span % 2)) * size
        mine = me % size
        spans.append((size, BLOCK >> b, sibling, mine))

    k_own = kv[0, HALO:FAR, :]
    v_own = kv[1, HALO:FAR, :]
    for b, (size, rows, sibling, mine) in enumerate(spans):
        if b < 3:
            mat = group_matrix((rows, ROWS), 1, rows, 0)
            psend[b][0] = dot_nn(mat, k_own).astype(BF16)
            psend[b][1] = dot_nn(mat, v_own).astype(BF16)
        else:
            mat = group_matrix((8, ROWS), 1, rows, (mine * rows) % 8)
            psend[b][...] = jnp.concatenate(
                [dot_nn(mat, k_own), dot_nn(mat, v_own)], axis=0
            ).astype(BF16)

    if levels > 4:
        pl.semaphore_wait(barrier, n_seq)
    else:
        greeted = n_seq // 2 + 1
        pl.when(has_across)(lambda: pl.semaphore_wait(barrier, greeted + 1))
        pl.when(jnp.logical_not(has_across))(lambda: pl.semaphore_wait(barrier, greeted))

    def halo_copy(way, h):
        if way == 0:
            src, dst, to = kv.at[:, HALO + BLOCK : FAR, part_of[h]], kv.at[:, 0:BLOCK, part_of[h]], me + 1
        else:
            src, dst, to = kv.at[:, HALO : HALO + BLOCK, part_of[h]], kv.at[:, BLOCK:HALO, part_of[h]], me - 1
        return pltpu.make_async_remote_copy(
            src, dst, halo_s.at[h, way], halo_r.at[h, way],
            device_id={"seq": to}, device_id_type=MESH,
        )

    relayed = list(range(1, min(levels, 4)))

    def count(b):
        return 2 ** (b - 1) if b in relayed else 2**b

    def key_rows(b, at, n, h):
        return kv.at[:, pl.ds(pl.multiple_of(FAR + BLOCK * b + at, 16), n), part_of[h]]

    def far_copy(b, dest, slot, h):
        size, rows, sibling, mine = spans[b]
        to = sibling + dest
        if b in relayed:
            slot = core * (size // 2) + slot
            to = sibling + 2 * dest + core
        if b < 3:
            src, dst = psend[b].at[:, :, part_of[h]], key_rows(b, slot * rows, rows, h)
        else:
            src, dst = psend[b].at[:, part_of[h]], srecv[b - 3].at[slot, :, part_of[h]]
        return pltpu.make_async_remote_copy(
            src, dst, far_s.at[h, size - 1 + dest], far_r.at[h, size - 1 + slot],
            device_id={"seq": to}, device_id_type=MESH,
        )

    def my_slot(b):
        return mine_of[b] // 2 if b in relayed else mine_of[b]

    mine_of = [span[3] for span in spans]

    def relay_copy(b, part, h):
        if b < 3:
            ref = key_rows(b, part * (BLOCK // 2), BLOCK // 2, h)
        else:
            ref = srecv[0].at[pl.ds(part * 4, 4), :, part_of[h]]
        return pltpu.make_async_remote_copy(
            ref, ref, relay_s.at[h, b], relay_r.at[h, b],
            device_id={"seq": twin}, device_id_type=MESH,
        )

    has_next = me < n_seq - 1
    has_prev = me > 0
    for h in range(2):
        for b in reversed(range(levels)):
            each(count(b), lambda i: far_copy(b, i, my_slot(b), h).start())
        pl.when(has_next)(lambda: halo_copy(0, h).start())
        pl.when(has_prev)(lambda: halo_copy(1, h).start())

    loads[2].wait()
    loads[3].wait()
    dattn[...] = dot_nt(dm[...], w[...]).astype(BF16)
    loads[4].wait()

    def hand_on(h):
        for b in reversed(relayed):
            each(count(b), lambda i: far_copy(b, 0, i, h).wait_recv())
            relay_copy(b, core, h).start()

    def place(b, slot):
        return (slot % 2) * 4 + slot // 2 if b == 3 else slot

    def collect(h):
        pl.when(has_prev)(lambda: halo_copy(0, h).wait_recv())
        pl.when(has_next)(lambda: halo_copy(1, h).wait_recv())
        for b in range(levels):
            if b in relayed:
                relay_copy(b, 1 - core, h).wait_recv()
            else:
                each(count(b), lambda i: far_copy(b, 0, i, h).wait_recv())
        for b in range(3, levels):
            per = 8 // spans[b][1]
            pieces = []
            for g in range(8):
                total = srecv[b - 3][place(b, g * per), :, part_of[h]].astype(F32)
                for s in range(1, per):
                    total = total + srecv[b - 3][g * per + s, :, part_of[h]].astype(F32)
                pieces.append(total)
            at = FAR + BLOCK * b
            for part in range(2):
                kv[part, at : at + BLOCK, part_of[h]] = jnp.concatenate(
                    [piece[8 * part : 8 * part + 8] for piece in pieces], axis=0
                ).astype(BF16)

    lane = lax.broadcasted_iota(jnp.int32, (1, PAIR), 1)
    head_a = jnp.where(lane < HEAD_DIM, 1.0, 0.0).astype(BF16)
    head_b = jnp.where(lane < HEAD_DIM, 0.0, 1.0).astype(BF16)
    token = (lax.broadcasted_iota(jnp.int32, (1, 2 * ROWS), 1) // BLOCK) % 2
    first = token == 0
    mask0 = jnp.where(first, 1.0, 0.0)
    mask1 = jnp.where(first, 0.0, 1.0)

    def attend(pair):
        cols = slice(pair * PAIR, (pair + 1) * PAIR)
        qp = q[:, cols] * jnp.asarray(0.125, BF16)
        dap = dattn[:, cols]
        qs = jnp.concatenate([qp * head_a, qp * head_b], axis=0)
        das = jnp.concatenate([dap * head_a, dap * head_b], axis=0)
        kp = kv[0, :, cols]
        vp = kv[1, :, cols]

        def merge(full):
            halo = jnp.where(first, full[:BLOCK], full[BLOCK:HALO])
            return halo, full[HALO:]

        s_halo, s_rest = merge(dot_nt(kp, qs))
        s_all = jnp.concatenate([s_halo + bias[0:1, :], s_rest], axis=0)
        top = jnp.max(s_all, axis=0, keepdims=True)
        e_all = jnp.exp(s_all - top)
        normed = e_all * (1.0 / jnp.sum(e_all, axis=0, keepdims=True))

        def unmerge(full):
            halo = full[:BLOCK]
            return jnp.concatenate(
                [halo * mask0, halo * mask1, full[BLOCK:]], axis=0
            ).astype(BF16)

        weights = unmerge(normed)
        d_halo, d_rest = merge(dot_nt(vp, das))
        d_normed = jnp.concatenate([d_halo, d_rest], axis=0)
        inner = jnp.sum(normed * d_normed, axis=0, keepdims=True)
        d_scores = unmerge(normed * (d_normed - inner))

        def both(values_t, coeffs):
            full = dot_nn(values_t, coeffs)
            return jnp.concatenate(
                [full[:HEAD_DIM, :ROWS], full[HEAD_DIM:, ROWS:]], axis=0
            ).T

        attn[:, cols] = both(vp.T, weights).astype(BF16)
        dq[:, cols] = (both(kp.T, d_scores) * 0.125).astype(BF16)
        grads = (dot_nn(d_scores, qs), dot_nn(weights, das))
        for part in range(2):
            grad = grads[part]
            hsend[part, :, cols] = grad[:HALO].astype(BF16)
            gown[part, :, cols] = grad[HALO:FAR]
            gsend[part, :, cols] = grad[FAR : FAR + BLOCK * big].astype(BF16)
        for b in range(3, levels):
            at = FAR + BLOCK * b
            for g in range(8):
                gssend[b - 3][place(b, g), :, cols] = jnp.concatenate(
                    [grad[at + 8 * g : at + 8 * g + 8] for grad in grads], axis=0
                ).astype(BF16)

    def ghalo_copy(way, h):
        if way == 0:
            src, dst, to = hsend.at[:, 0:BLOCK, part_of[h]], hrecv.at[:, BLOCK:HALO, part_of[h]], me - 1
        else:
            src, dst, to = hsend.at[:, BLOCK:HALO, part_of[h]], hrecv.at[:, 0:BLOCK, part_of[h]], me + 1
        return pltpu.make_async_remote_copy(
            src, dst, ghalo_s.at[h, way], ghalo_r.at[h, way],
            device_id={"seq": to}, device_id_type=MESH,
        )

    def sum_copy(b, h):
        half = BLOCK // 2
        if b < 3:
            at = BLOCK * b + (1 - core) * half
            src = gsend.at[:, pl.ds(pl.multiple_of(at, half), half), part_of[h]]
            dst = sum_recv.at[:, half * (b - 1) : half * b, part_of[h]]
        else:
            src = gssend[0].at[pl.ds((1 - core) * 4, 4), :, part_of[h]]
            dst = small_recv.at[:, :, part_of[h]]
        return pltpu.make_async_remote_copy(
            src, dst, sum_s.at[h, b], sum_r.at[h, b],
            device_id={"seq": twin}, device_id_type=MESH,
        )

    def gfar_copy(b, dest, slot, h):
        size, rows, sibling, mine = spans[b]
        to = sibling + dest
        if b == 0:
            src, dst = gsend.at[:, 0:BLOCK, part_of[h]], grecv.at[:, 0:BLOCK, part_of[h]]
        elif b < 3:
            half = BLOCK // 2
            src = sum_send.at[:, pl.ds(pl.multiple_of(half * (b - 1) + dest * rows, 16), rows), part_of[h]]
            dst = grecv.at[:, pl.ds(pl.multiple_of(half * (b + 1) + slot * rows, 16), rows), part_of[h]]
        elif b == 3:
            src, dst = small_send.at[dest, :, part_of[h]], gsrecv[0].at[slot, :, part_of[h]]
        else:
            src = gssend[b - 3].at[dest // (8 // rows), :, part_of[h]]
            dst = gsrecv[b - 3].at[slot, :, part_of[h]]
        if b in relayed:
            to = sibling + 2 * dest + core
        return pltpu.make_async_remote_copy(
            src, dst, gfar_s.at[h, size - 1 + dest], gfar_r.at[h, size - 1 + slot],
            device_id={"seq": to}, device_id_type=MESH,
        )

    def give_back(h):
        for b in reversed(relayed):
            sum_copy(b, h).start()
        pl.when(has_prev)(lambda: ghalo_copy(0, h).start())
        pl.when(has_next)(lambda: ghalo_copy(1, h).start())
        for b in range(levels):
            if b not in relayed:
                each(count(b), lambda i: gfar_copy(b, i, my_slot(b), h).start())

    def give_back_sums(h):
        half = BLOCK // 2
        for b in reversed(relayed):
            sum_copy(b, h).wait_recv()
            if b < 3:
                mine_rows = pl.ds(pl.multiple_of(BLOCK * b + core * half, half), half)
                own = gsend[:, mine_rows, part_of[h]].astype(F32)
                theirs = sum_recv[:, half * (b - 1) : half * b, part_of[h]].astype(F32)
                sum_send[:, half * (b - 1) : half * b, part_of[h]] = (own + theirs).astype(BF16)
            else:
                own = gssend[0][pl.ds(core * 4, 4), :, part_of[h]].astype(F32)
                theirs = small_recv[:, :, part_of[h]].astype(F32)
                small_send[:, :, part_of[h]] = (own + theirs).astype(BF16)
            each(count(b), lambda i: gfar_copy(b, i, my_slot(b), h).start())

    pairs = feats // PAIR // 2
    hand_on(0)
    collect(0)
    for pair in range(pairs):
        attend(pair)
        if pair == 0:
            hand_on(1)
    give_back(0)
    collect(1)
    for pair in range(pairs, 2 * pairs):
        attend(pair)
        if pair == pairs:
            give_back_sums(0)
    give_back(1)

    theirs = pl.ds(pl.multiple_of(other_head * BLOCK, BLOCK), BLOCK)
    ours = pl.ds(pl.multiple_of(hd * BLOCK, BLOCK), BLOCK)
    mix_send[...] = dot_nn(attn[theirs, :], w[...]).astype(BF16)
    mix_copy = pltpu.make_async_remote_copy(
        mix_send, mix_recv, mix_sem.at[0], mix_sem.at[1],
        device_id={"head": other_head}, device_id_type=MESH,
    )
    mix_copy.start()
    give_back_sums(1)
    mix_own[...] = dot_nn(attn[ours, :], w[...])

    for h in range(2):
        pl.when(has_next)(lambda: ghalo_copy(0, h).wait_recv())
        pl.when(has_prev)(lambda: ghalo_copy(1, h).wait_recv())
        for b in range(levels):
            each(count(b), lambda i: gfar_copy(b, 0, i, h).wait_recv())
        for part in range(2):
            total = gown[part, :, part_of[h]] + hrecv[part, :, part_of[h]].astype(F32)
            for b, (size, rows, sibling, mine) in enumerate(spans):
                group = ROWS // rows
                wide = (rows if b < 3 else 16) * count(b)
                token = lax.broadcasted_iota(jnp.int32, (ROWS, wide), 0)
                row = lax.broadcasted_iota(jnp.int32, (ROWS, wide), 1)
                if b < 3:
                    at = BLOCK // 2 * (b + 1) if b else 0
                    same = token // group == row % rows
                    got = grecv[part, at : at + wide, part_of[h]]
                else:
                    same = token // group + (mine * rows) % 8 + 8 * part == row % 16
                    got = gsrecv[b - 3][:, :, part_of[h]].reshape(wide, feats // 2)
                mat = jnp.where(same, 1.0 / group, 0.0).astype(BF16)
                total = total + dot_nn(mat, got)
            (dk_out, dv_out)[part][:, part_of[h]] = total.astype(BF16)

    mix_copy.wait_recv()
    mixed_out[...] = (mix_own[...] + mix_recv[...].astype(F32)).astype(BF16)

    for h in range(2):
        pl.when(has_next)(lambda: halo_copy(0, h).wait_send())
        pl.when(has_prev)(lambda: halo_copy(1, h).wait_send())
        pl.when(has_prev)(lambda: ghalo_copy(0, h).wait_send())
        pl.when(has_next)(lambda: ghalo_copy(1, h).wait_send())
        for b in range(levels):
            each(count(b), lambda i: far_copy(b, i, my_slot(b), h).wait_send())
            each(count(b), lambda i: gfar_copy(b, i, my_slot(b), h).wait_send())
        for b in relayed:
            relay_copy(b, core, h).wait_send()
            sum_copy(b, h).wait_send()
    mix_copy.wait_send()


def write_kernel(*refs):
    in_sem, out_sem = refs[12:]
    reads = [pltpu.make_async_copy(refs[i], refs[8 + i], in_sem.at[i]) for i in range(4)]
    writes = [pltpu.make_async_copy(refs[8 + i], refs[4 + i], out_sem.at[i]) for i in range(4)]
    for read in reads:
        read.start()
    for read, write in zip(reads, writes):
        read.wait()
        write.start()
    for write in writes:
        write.wait()


def on_device(n_seq, queries, keys, values, w_out, d_mixed):
    feats = queries.shape[1]
    width = w_out.shape[1]
    levels = n_seq.bit_length() - 1
    big = min(levels, 3)
    small = list(range(3, levels))
    n_keys = FAR + BLOCK * levels
    vmem = pltpu.VMEM
    dma = pltpu.SemaphoreType.DMA
    scratch = [
        vmem((ROWS, feats), BF16),
        vmem((feats, width), BF16),
        vmem((ROWS, width), BF16),
        vmem((2, n_keys, feats), BF16),
        vmem((ROWS, feats), BF16),
        vmem((ROWS, feats), BF16),
        vmem((8, 2 * ROWS), F32),
        vmem((2, ROWS, feats), F32),
        vmem((2, HALO, feats), BF16),
        vmem((2, HALO, feats), BF16),
        vmem((2, BLOCK * big, feats), BF16),
        vmem((2, 2 * BLOCK, feats), BF16),
        vmem((BLOCK, width), BF16),
        vmem((BLOCK, width), BF16),
        vmem((BLOCK, width), F32),
        dma((5,)),
        dma((2, 2)),
        dma((2, 2)),
        dma((2, n_seq - 1)),
        dma((2, n_seq - 1)),
        dma((2, 2)),
        dma((2, 2)),
        dma((2, n_seq - 1)),
        dma((2, n_seq - 1)),
        dma((2,)),
        dma((2, 4)),
        dma((2, 4)),
        dma((2, 4)),
        dma((2, 4)),
        vmem((2, BLOCK, feats), BF16),
        vmem((2, BLOCK, feats), BF16),
        vmem((4, 16, feats), BF16),
        vmem((4, 16, feats), BF16),
    ]
    scratch += [vmem((2, BLOCK >> b, feats), BF16) for b in range(big)]
    scratch += [vmem((16, feats), BF16) for b in small]
    scratch += [vmem((2**b, 16, feats), BF16) for b in small]
    scratch += [vmem((8, 16, feats), BF16) for b in small]
    scratch += [vmem((2**b // (2 if b == 3 else 1), 16, feats), BF16) for b in small]
    in_hbm = pl.BlockSpec(memory_space=pltpu.HBM)
    in_vmem = pl.BlockSpec(memory_space=pltpu.VMEM)
    shapes = [
        jax.ShapeDtypeStruct((BLOCK, width), BF16),
        jax.ShapeDtypeStruct((ROWS, feats), BF16),
        jax.ShapeDtypeStruct((ROWS, feats), BF16),
        jax.ShapeDtypeStruct((ROWS, feats), BF16),
    ]
    results = pl.pallas_call(
        functools.partial(kernel, n_seq, levels),
        out_shape=shapes,
        in_specs=[in_hbm] * 5,
        out_specs=[in_vmem] * 4,
        scratch_shapes=scratch,
        compiler_params=pltpu.CompilerParams(
            collective_id=0, has_side_effects=True, vmem_limit_bytes=63 * 2**20
        ),
    )(queries, keys, values, w_out, d_mixed)
    return pl.pallas_call(
        write_kernel,
        out_shape=shapes,
        in_specs=[in_hbm] * 4,
        out_specs=[in_hbm] * 4,
        scratch_shapes=[vmem(s.shape, s.dtype) for s in shapes] + [dma((4,)), dma((4,))],
        compiler_params=pltpu.CompilerParams(vmem_limit_bytes=63 * 2**20),
    )(*results)


def solution(mesh):
    in_specs = (
        P("seq", "head"),
        P("seq", "head"),
        P("seq", "head"),
        P("head", None),
        P("seq", None),
    )
    out_specs = (P(("seq", "head"), None), P("seq", "head"), P("seq", "head"), P("seq", "head"))
    return jax.shard_map(
        functools.partial(on_device, mesh.shape["seq"]),
        mesh=mesh,
        in_specs=in_specs,
        out_specs=out_specs,
        check_vma=False,
    )
```
